1024 devices in a mesh: dp: 16 (over z_hi, y), expert: 64 (over z_lo, x, core).
Axes of the slice: x: 4, y: 4, z: 32 (z_hi: 4, z_lo: 8; z = z_hi * 8 + z_lo), core: 2. Of those that a mesh axis runs over, the one named last changes fastest.
Arguments:
- grad_out: bfloat16 [131072, 4096], P(('dp', 'expert')), may hold values from -2 to 2
- expert_ids: int32 [131072], P(('dp', 'expert')), may hold values from 0 to 63, as said below
- gate_weight: bfloat16 [131072], P(('dp', 'expert')), may hold values from 0.099609375 to 1
- saved_hidden: bfloat16 [16, 64, 192, 768], P('dp', 'expert'), may hold values from -6 to 6
- down_weight: bfloat16 [64, 768, 4096], P('expert'), may hold values from -0.21875 to 0.21875
- adapter_a: bfloat16 [64, 32, 768], P('expert'), may hold values from -0.21875 to 0.21875
- adapter_b: bfloat16 [64, 32, 4096], P('expert'), may hold values from -1 to 1
Outputs:
- hidden_gradient: bfloat16 [16, 64, 192, 768], P('dp', 'expert')
- gate_grad: float32 [131072], P(('dp', 'expert'))
- adapter_a_grad: float32 [64, 32, 768], P('expert')
- adapter_b_grad: float32 [64, 32, 4096], P('expert')
The draws below stay inside these ranges and needn't reach their ends.
Inputs may be any that keep to these rules, and one draw needn't show every extreme that they name: `expert_ids`: in each block of 128 tokens that one device holds, no expert is named by more than 3 tokens, and one expert, drawn from the seed, is named by exactly 3 tokens in every block.
All inputs are finite; a program needn't handle non-finite values.
Results may differ from the reference program's by a relative error of at most 0.0049.
Values may be sent and summed in bfloat16 or wider, within the bound.
No kernel may reach another device: no remote copies, remote signals or barrier semaphores. Data moves between devices by JAX's collectives and lax.ppermute only.
A program may use at most 64 MiB of HBM per device.

```python
import math
from functools import partial
import jax
import jax.numpy as jnp
from jax import lax

D = 4096
F = 768
RANK = 32
TOK_DEV = 128
EXPERTS = 64
CAP = 3
TOKENS = 131072
N_DP = 16
DEVICES = 1024


def draw_expert_ids(key, part):
    key = jax.random.fold_in(key, 5)
    ranking = jax.random.permutation(jax.random.fold_in(key, 1), EXPERTS)
    popular = max(EXPERTS // 8, 1)
    tier = jnp.where(ranking == 0, 2, jnp.where(ranking < popular, 1, 0)).astype(jnp.int32)
    total_slots = EXPERTS * CAP
    slot_tier = jnp.repeat(tier, CAP)
    slot_ids = jnp.arange(total_slots, dtype=jnp.int32)

    def one_block(index):
        block_key = jax.random.fold_in(key, index + 2)
        noise = jax.random.randint(jax.random.fold_in(block_key, 0), (total_slots,), 0, 16384, dtype=jnp.int32)
        score = (slot_tier * 32768 + noise) * 4096 + slot_ids
        picked = lax.top_k(score, TOK_DEV)[1]
        chosen = (picked // CAP).astype(jnp.int32)
        return jax.random.permutation(jax.random.fold_in(block_key, 1), chosen)
    return jax.vmap(one_block)(jnp.arange(DEVICES, dtype=jnp.int32)).reshape(-1)


def block_levels(own_key, dims, cuts, smallest, top_value):
    gain, own = 1.0, jax.random.fold_in(own_key, 6)
    for dim, blocks in cuts:
        heights = jnp.exp(jax.random.uniform(jax.random.fold_in(own, dim), (blocks,), jnp.float32, smallest / len(cuts), top_value / len(cuts)))
        gain = gain * jnp.repeat(heights, dims[dim] // blocks).reshape([-1 if axis == dim else 1 for axis in range(len(dims))])
    return gain


def scatter_about(own_key, extent, spread, limit, split=(), kind=jnp.bfloat16):
    result = jax.random.normal(own_key, extent, jnp.float32) * spread
    if len(split) > 0:
        result = block_levels(own_key, extent, split, -0.22, 0.18) * result
    return jnp.clip(result, min=-limit, max=limit).astype(kind)


def setup_inputs(seed: int = 0) -> dict:
    key_of = jax.random.split(jax.random.key(seed), 8)
    grad_out = scatter_about(key_of[0], (TOKENS, D), 0.25, 2.0, ((0, 1024),))
    expert_ids = draw_expert_ids(jax.random.fold_in(key_of[7], 71), 0)
    gate_weight = jnp.clip(jnp.exp(math.log(1.0) - 2.306499 * jax.random.uniform(key_of[2], (TOKENS,), jnp.float32) ** block_levels(key_of[2], (TOKENS,), ((0, 1024),), -0.2, 0.2)), 0.099609375, 1.0).astype(jnp.bfloat16)
    saved_hidden = scatter_about(key_of[3], (N_DP, EXPERTS, EXPERTS * CAP, F), 1.0, 6.0, ((0, 16), (1, 64)))
    down_weight = scatter_about(key_of[4], (EXPERTS, F, D), F ** -0.5, 0.21875, ((0, 64),))
    adapter_a = scatter_about(key_of[5], (EXPERTS, RANK, F), F ** -0.5, 0.21875, ((0, 64),))
    adapter_b = scatter_about(key_of[6], (EXPERTS, RANK, D), RANK ** -0.5, 1.0, ((0, 64),))
    return dict(grad_out=grad_out, expert_ids=expert_ids, gate_weight=gate_weight, saved_hidden=saved_hidden, down_weight=down_weight, adapter_a=adapter_a, adapter_b=adapter_b)


adapter_scale = 2.0


def slot_tokens(expert_ids):
    blocks = expert_ids.reshape(N_DP, EXPERTS, TOK_DEV)
    labels = jnp.arange(EXPERTS, dtype=jnp.int32)
    onehot = (blocks[..., None] == labels).astype(jnp.int32)
    token_rank = jnp.sum((jnp.cumsum(onehot, axis=2) - onehot) * onehot, axis=3)
    replica = jnp.arange(N_DP, dtype=jnp.int32)[:, None, None]
    source = jnp.arange(EXPERTS, dtype=jnp.int32)[None, :, None]
    within = jnp.arange(TOK_DEV, dtype=jnp.int32)[None, None, :]
    position = ((replica * EXPERTS + blocks) * EXPERTS + source) * CAP + token_rank
    token_id = (replica * EXPERTS + source) * TOK_DEV + within
    table = jnp.full((N_DP * EXPERTS * EXPERTS * CAP,), -1, jnp.int32)
    table = table.at[position.reshape(-1)].set(token_id.reshape(-1))
    return table.reshape(N_DP, EXPERTS, EXPERTS * CAP)


def one_expert(grad_out, gate_weight, pieces):
    token_ids, hidden_activation_rows, weight, factor_a, second_factor = pieces
    token_ids = token_ids.reshape(-1)
    valid = token_ids >= 0
    safe_ids = jnp.maximum(token_ids, 0)
    grad_rows = jnp.where(valid[:, None], grad_out[safe_ids], 0).astype(jnp.bfloat16)
    gate_values = jnp.where(valid, gate_weight[safe_ids].astype(jnp.float32), 0.0).astype(jnp.float32)
    hidden_activation_rows = hidden_activation_rows.reshape(-1, hidden_activation_rows.shape[-1])
    reduced_rank_rows = jnp.dot(hidden_activation_rows, factor_a.T, preferred_element_type=jnp.float32).astype(jnp.bfloat16)
    projected_rows = jnp.dot(grad_rows, weight.T, preferred_element_type=jnp.float32)
    adapter_proj = jnp.dot(grad_rows, second_factor.T, preferred_element_type=jnp.float32)
    rounded_proj = adapter_proj.astype(jnp.bfloat16)
    backward_product = jnp.dot(rounded_proj, factor_a, preferred_element_type=jnp.float32)
    hidden_gradient = (gate_values[:, None] * (projected_rows + adapter_scale * backward_product)).astype(jnp.bfloat16)
    output_gradient_rows = jnp.dot(hidden_activation_rows, weight, preferred_element_type=jnp.float32)
    output_gradient_rows = output_gradient_rows + adapter_scale * jnp.dot(reduced_rank_rows, second_factor, preferred_element_type=jnp.float32)
    gate_terms = jnp.sum(grad_rows.astype(jnp.float32) * output_gradient_rows, axis=1)
    gate_scaled_rows = (gate_values[:, None] * grad_rows.astype(jnp.float32)).astype(jnp.bfloat16)
    second_factor_gradient = adapter_scale * jnp.dot(reduced_rank_rows.T, gate_scaled_rows, preferred_element_type=jnp.float32)
    scaled_projection = (gate_values[:, None] * adapter_proj).astype(jnp.bfloat16)
    first_factor_gradient = adapter_scale * jnp.dot(scaled_projection.T, hidden_activation_rows, preferred_element_type=jnp.float32)
    return hidden_gradient, gate_terms, first_factor_gradient, second_factor_gradient


def reference(grad_out, expert_ids, gate_weight, saved_hidden, down_weight, adapter_a, adapter_b):
    table = jnp.swapaxes(slot_tokens(expert_ids), 0, 1)
    pieces = (table, jnp.swapaxes(saved_hidden, 0, 1), down_weight, adapter_a, adapter_b)
    hidden_gradient, gate_terms, first_factor_gradient, second_factor_gradient = lax.map(partial(one_expert, grad_out, gate_weight), pieces)
    flat_ids = table.reshape(-1)
    total = N_DP * EXPERTS * TOK_DEV
    target = jnp.where(flat_ids >= 0, flat_ids, total).astype(jnp.int32)
    gate_grad = jnp.zeros((total,), jnp.float32).at[target].set(gate_terms.reshape(-1), mode="drop")
    hidden_gradient = jnp.swapaxes(hidden_gradient.reshape(EXPERTS, N_DP, EXPERTS * CAP, -1), 0, 1)
    return hidden_gradient, gate_grad, first_factor_gradient, second_factor_gradient
```

```python
import jax
import jax.numpy as jnp
from jax import lax
from jax.sharding import PartitionSpec as P

adapter_scale = 2.0
Y_SIZE = 4


def dp_groups():
    z_count = lax.axis_size("dp") // Y_SIZE
    along_y = [[z * Y_SIZE + y for y in range(Y_SIZE)] for z in range(z_count)]
    along_z = [[z * Y_SIZE + y for z in range(z_count)] for y in range(Y_SIZE)]
    return along_y, along_z


def exchange(blocks, axis, groups=None):
    return lax.all_to_all(blocks, axis, split_axis=0, concat_axis=0, tiled=True, axis_index_groups=groups)


def sum_over_dp(part):
    along_y, along_z = dp_groups()
    rank, columns = part.shape
    mine = part.astype(jnp.bfloat16).reshape(Y_SIZE, rank // Y_SIZE, columns)
    summed = jnp.sum(exchange(mine, "dp", along_y).astype(jnp.float32), axis=0)
    copies = jnp.broadcast_to(summed.astype(jnp.bfloat16)[None], (len(along_z[0]),) + summed.shape)
    summed = jnp.sum(exchange(copies, "dp", along_z).astype(jnp.float32), axis=0)
    copies = jnp.broadcast_to(summed.astype(jnp.bfloat16)[None], (Y_SIZE,) + summed.shape)
    return exchange(copies, "dp", along_y).reshape(rank, columns)


def shards(grad_out, expert_ids, gate_weight, saved_hidden, down_weight, adapter_a, adapter_b):
    experts = lax.axis_size("expert")
    capacity = saved_hidden.shape[2] // experts
    slots = experts * capacity
    width = grad_out.shape[1]
    hidden_width = saved_hidden.shape[3]
    gates = gate_weight.astype(jnp.float32)
    labels = jnp.arange(experts, dtype=jnp.int32)
    onehot = (expert_ids[:, None] == labels[None, :]).astype(jnp.int32)
    token_rank = jnp.sum((jnp.cumsum(onehot, axis=0) - onehot) * onehot, axis=1)
    slot_index = expert_ids * capacity + token_rank
    chosen = jnp.arange(slots, dtype=jnp.int32)[:, None] == slot_index[None, :]
    scaled = (gates[:, None] * grad_out.astype(jnp.float32)).astype(jnp.bfloat16)
    outgoing = jnp.dot(chosen.astype(jnp.bfloat16), scaled, preferred_element_type=jnp.float32).astype(jnp.bfloat16)
    arrived = exchange(outgoing.reshape(experts, capacity * 8, width // 8), "expert")
    rows = arrived.reshape(slots, width)

    hidden = saved_hidden.reshape(slots, hidden_width)
    weight, factor_a, factor_b = down_weight[0], adapter_a[0], adapter_b[0]
    low_rank = jnp.dot(hidden, factor_a.T, preferred_element_type=jnp.float32).astype(jnp.bfloat16)
    over_columns = (((1,), (1,)), ((), ()))
    over_slots = (((0,), (0,)), ((), ()))
    adapter_proj = lax.dot_general(rows, factor_b, over_columns, preferred_element_type=jnp.float32)
    rounded_proj = adapter_proj.astype(jnp.bfloat16)
    part_b = adapter_scale * lax.dot_general(low_rank, rows, over_slots, preferred_element_type=jnp.float32)
    part_a = adapter_scale * lax.dot_general(rounded_proj, hidden, over_slots, preferred_element_type=jnp.float32)
    summed = sum_over_dp(jnp.concatenate([part_b, part_a], axis=1)).astype(jnp.float32)

    projected = lax.dot_general(rows, weight, over_columns, preferred_element_type=jnp.float32)
    back = jnp.dot(rounded_proj, factor_a, preferred_element_type=jnp.float32)
    hidden_gradient = (projected + adapter_scale * back).astype(jnp.bfloat16)
    gate_terms = jnp.sum(hidden.astype(jnp.float32) * projected, axis=1)
    gate_terms = gate_terms + adapter_scale * jnp.sum(low_rank.astype(jnp.float32) * adapter_proj, axis=1)
    came_back = exchange(gate_terms.reshape(experts, capacity), "expert").reshape(-1)
    gate_grad = jnp.sum(jnp.where(chosen, came_back[:, None], 0.0), axis=0) / gates
    return (hidden_gradient.reshape(saved_hidden.shape), gate_grad, summed[None, :, width:], summed[None, :, :width])


def solution(mesh):
    in_specs = (
        P(("dp", "expert"), None),
        P(("dp", "expert")),
        P(("dp", "expert")),
        P("dp", "expert", None, None),
        P("expert", None, None),
        P("expert", None, None),
        P("expert", None, None),
    )
    out_specs = (
        P("dp", "expert", None, None),
        P(("dp", "expert")),
        P("expert", None, None),
        P("expert", None, None),
    )
    return jax.shard_map(shards, mesh=mesh, in_specs=in_specs, out_specs=out_specs, check_vma=False)
```

```python
import jax
import jax.numpy as jnp
from jax import lax
from jax.sharding import PartitionSpec as P

adapter_scale = 2.0
Y_SIZE = 4


def exchange(blocks, axis, groups=None):
    return lax.all_to_all(blocks, axis, split_axis=0, concat_axis=0, tiled=True, axis_index_groups=groups)


def y_groups():
    z_count = lax.axis_size("dp") // Y_SIZE
    return [[z * Y_SIZE + y for y in range(Y_SIZE)] for z in range(z_count)]


def narrow(values):
    return lax.reduce_precision(values, exponent_bits=8, mantissa_bits=7)


def head_and_rest(values, split):
    tail = values[:, split:]
    head = narrow(tail)
    return jnp.concatenate([narrow(values[:, :split]), head, narrow(tail - head)], axis=1)


def joined(values, split):
    middle = split + (values.shape[1] - split) // 2
    return jnp.concatenate([values[:, :split], values[:, split:middle] + values[:, middle:]], axis=1)


def sum_over_y(part, split):
    rank = part.shape[0]
    mine = head_and_rest(part, split).astype(jnp.bfloat16).reshape(Y_SIZE, rank // Y_SIZE, -1)
    return joined(jnp.sum(exchange(mine, "dp", y_groups()).astype(jnp.float32), axis=0), split)


def sum_over_z(part, split):
    z_count = lax.axis_size("dp") // Y_SIZE
    for mask in (1, z_count - 1):
        pairs = [(z * Y_SIZE + y, (z ^ mask) * Y_SIZE + y) for z in range(z_count) for y in range(Y_SIZE)]
        own = head_and_rest(part, split)
        other = lax.ppermute(own.astype(jnp.bfloat16), "dp", pairs)
        part = joined(own + other.astype(jnp.float32), split)
    return part


def gather_over_y(part):
    copies = jnp.broadcast_to(part.astype(jnp.bfloat16)[None], (Y_SIZE,) + part.shape)
    return exchange(copies, "dp", y_groups()).reshape(-1, part.shape[1])


def shards(grad_out, expert_ids, gate_weight, saved_hidden, down_weight, adapter_a, adapter_b):
    experts = lax.axis_size("expert")
    capacity = saved_hidden.shape[2] // experts
    slots = experts * capacity
    width = grad_out.shape[1]
    hidden_width = saved_hidden.shape[3]
    gates = gate_weight.astype(jnp.float32)
    labels = jnp.arange(experts, dtype=jnp.int32)
    onehot = (expert_ids[:, None] == labels[None, :]).astype(jnp.int32)
    token_rank = jnp.sum((jnp.cumsum(onehot, axis=0) - onehot) * onehot, axis=1)
    slot_index = expert_ids * capacity + token_rank
    chosen = jnp.arange(slots, dtype=jnp.int32)[:, None] == slot_index[None, :]
    scaled = (gates[:, None] * grad_out.astype(jnp.float32)).astype(jnp.bfloat16)
    outgoing = jnp.dot(chosen.astype(jnp.bfloat16), scaled, preferred_element_type=jnp.float32).astype(jnp.bfloat16)
    arrived = exchange(outgoing.reshape(experts, capacity * 8, width // 8), "expert")
    rows = arrived.reshape(slots, width)

    hidden = saved_hidden.reshape(slots, hidden_width)
    weight, factor_a, factor_b = down_weight[0], adapter_a[0], adapter_b[0]
    low_rank = jnp.dot(hidden, factor_a.T, preferred_element_type=jnp.float32).astype(jnp.bfloat16)
    over_columns = (((1,), (1,)), ((), ()))
    over_slots = (((0,), (0,)), ((), ()))
    adapter_proj = lax.dot_general(rows, factor_b, over_columns, preferred_element_type=jnp.float32)
    rounded_proj = adapter_proj.astype(jnp.bfloat16)
    part_b = adapter_scale * lax.dot_general(low_rank, rows, over_slots, preferred_element_type=jnp.float32)
    part_a = adapter_scale * lax.dot_general(rounded_proj, hidden, over_slots, preferred_element_type=jnp.float32)
    over_y = sum_over_y(jnp.concatenate([part_b, part_a], axis=1), width)
    summed = gather_over_y(sum_over_z(over_y, width)).astype(jnp.float32)

    projected = lax.dot_general(rows, weight, over_columns, preferred_element_type=jnp.float32)
    back = jnp.dot(rounded_proj, factor_a, preferred_element_type=jnp.float32)
    hidden_gradient = (projected + adapter_scale * back).astype(jnp.bfloat16)
    gate_terms = jnp.sum(hidden.astype(jnp.float32) * projected, axis=1)
    gate_terms = gate_terms + adapter_scale * jnp.sum(low_rank.astype(jnp.float32) * adapter_proj, axis=1)
    gate_terms, _ = lax.optimization_barrier((gate_terms, over_y))
    came_back = exchange(gate_terms.reshape(experts, capacity), "expert").reshape(-1)
    gate_grad = jnp.sum(jnp.where(chosen, came_back[:, None], 0.0), axis=0) / gates
    return (hidden_gradient.reshape(saved_hidden.shape), gate_grad, summed[None, :, width:], summed[None, :, :width])


def solution(mesh):
    in_specs = (
        P(("dp", "expert"), None),
        P(("dp", "expert")),
        P(("dp", "expert")),
        P("dp", "expert", None, None),
        P("expert", None, None),
        P("expert", None, None),
        P("expert", None, None),
    )
    out_specs = (
        P("dp", "expert", None, None),
        P(("dp", "expert")),
        P("expert", None, None),
        P("expert", None, None),
    )
    return jax.shard_map(shards, mesh=mesh, in_specs=in_specs, out_specs=out_specs, check_vma=False)
```

```python
from functools import partial

import jax
import jax.numpy as jnp
from jax import lax
from jax.experimental import pallas as pl
from jax.experimental.pallas import tpu as pltpu
from jax.sharding import PartitionSpec as P

adapter_scale = 2.0
Y_SIZE = 4
SUBLANES = 8
LANES = 128
GRAD_PARTS = 4


def pack_kernel(capacity, ids_hbm, gate_hbm, grad_hbm, packed_ref, slot_ref, ids_ref, gate_ref, grad_ref, spread, sems):
    tokens, width = grad_ref.shape
    pieces, packed_rows, lanes = spread.shape
    slots = packed_rows // SUBLANES
    piece = width // SUBLANES
    small = [
        pltpu.make_async_copy(ids_hbm, ids_ref, sems.at[0]),
        pltpu.make_async_copy(gate_hbm, gate_ref, sems.at[1]),
    ]
    large = []
    for part in range(GRAD_PARTS):
        columns = pl.ds(part * (width // GRAD_PARTS), width // GRAD_PARTS)
        large.append(pltpu.make_async_copy(grad_hbm.at[:, columns], grad_ref.at[:, columns], sems.at[2 + part]))
    for copy in small + large:
        copy.start()
    for copy in small:
        copy.wait()
    ids = ids_ref[...]
    onehot = (lax.broadcasted_iota(jnp.int32, (slots // capacity, tokens), 0) == ids).astype(jnp.float32)
    earlier = lax.broadcasted_iota(jnp.int32, (tokens, tokens), 0) < lax.broadcasted_iota(jnp.int32, (tokens, tokens), 1)
    counts = jnp.dot(
        onehot.astype(jnp.bfloat16), earlier.astype(jnp.bfloat16), preferred_element_type=jnp.float32
    )
    token_rank = jnp.sum(onehot * counts, axis=0, keepdims=True).astype(jnp.int32)
    slot = ids * capacity + token_rank
    slot_ref[...] = slot
    gates = gate_ref[...].astype(jnp.float32)
    chosen = lax.broadcasted_iota(jnp.int32, (slots, tokens), 0) == slot
    select = jnp.where(chosen, gates, 0.0).astype(jnp.bfloat16)
    for j in range(SUBLANES):
        if j % (SUBLANES // GRAD_PARTS) == 0:
            large[j // (SUBLANES // GRAD_PARTS)].wait()
        rows = jnp.dot(select, grad_ref[:, j * piece : (j + 1) * piece], preferred_element_type=jnp.float32)
        for c in range(pieces):
            spread[c, pl.ds(j, slots, stride=SUBLANES), :] = rows[:, c * lanes : (c + 1) * lanes]
    for c in range(pieces):
        packed_ref[:, c * lanes : (c + 1) * lanes] = spread[c].astype(jnp.bfloat16)


def pack_rows(grad_out, expert_ids, gate_weight, slots, capacity):
    tokens, width = grad_out.shape
    piece = width // SUBLANES
    whole = pl.BlockSpec(memory_space=pltpu.VMEM)
    return pl.pallas_call(
        partial(pack_kernel, capacity),
        out_shape=(
            jax.ShapeDtypeStruct((slots * SUBLANES, piece), jnp.bfloat16),
            jax.ShapeDtypeStruct((1, tokens), jnp.int32),
        ),
        in_specs=[pl.BlockSpec(memory_space=pltpu.HBM)] * 3,
        out_specs=(whole, whole),
        scratch_shapes=[
            pltpu.VMEM((1, tokens), jnp.int32),
            pltpu.VMEM((1, tokens), jnp.bfloat16),
            pltpu.VMEM((tokens, width), jnp.bfloat16),
            pltpu.VMEM((piece // LANES, slots * SUBLANES, LANES), jnp.float32),
            pltpu.SemaphoreType.DMA((2 + GRAD_PARTS,)),
        ],
        compiler_params=pltpu.CompilerParams(vmem_limit_bytes=60 * 1024 * 1024),
        name="pack_rows",
    )(expert_ids.reshape(1, tokens), gate_weight.reshape(1, tokens), grad_out)


def exchange(blocks, axis, groups=None):
    return lax.all_to_all(blocks, axis, split_axis=0, concat_axis=0, tiled=True, axis_index_groups=groups)


def y_groups():
    z_count = lax.axis_size("dp") // Y_SIZE
    return [[z * Y_SIZE + y for y in range(Y_SIZE)] for z in range(z_count)]


def narrow(values):
    return lax.reduce_precision(values, exponent_bits=8, mantissa_bits=7)


def sum_over_y(part):
    rank = part.shape[0]
    mine = part.astype(jnp.bfloat16).reshape(Y_SIZE, rank // Y_SIZE, -1)
    return jnp.sum(exchange(mine, "dp", y_groups()).astype(jnp.float32), axis=0)


def pair_sum(part, mask):
    z_count = lax.axis_size("dp") // Y_SIZE
    pairs = [(z * Y_SIZE + y, (z ^ mask) * Y_SIZE + y) for z in range(z_count) for y in range(Y_SIZE)]
    own = narrow(part)
    other = lax.ppermute(own.astype(jnp.bfloat16), "dp", pairs)
    return own + other.astype(jnp.float32)


def gather_over_y(part):
    copies = jnp.broadcast_to(part.astype(jnp.bfloat16)[None], (Y_SIZE,) + part.shape)
    return exchange(copies, "dp", y_groups()).reshape(-1, part.shape[1])


def shards(grad_out, expert_ids, gate_weight, saved_hidden, down_weight, adapter_a, adapter_b):
    experts = lax.axis_size("expert")
    capacity = saved_hidden.shape[2] // experts
    slots = experts * capacity
    width = grad_out.shape[1]
    hidden_width = saved_hidden.shape[3]
    gates = gate_weight.astype(jnp.float32)
    packed, slot_index = pack_rows(grad_out, expert_ids, gate_weight, slots, capacity)
    arrived = exchange(packed.reshape(experts, capacity * SUBLANES, width // SUBLANES), "expert")
    rows = arrived.reshape(slots, width)

    hidden = saved_hidden.reshape(slots, hidden_width)
    weight, factor_a, factor_b = down_weight[0], adapter_a[0], adapter_b[0]
    low_rank = jnp.dot(hidden, factor_a.T, preferred_element_type=jnp.float32).astype(jnp.bfloat16)
    over_columns = (((1,), (1,)), ((), ()))
    over_slots = (((0,), (0,)), ((), ()))
    adapter_proj = lax.dot_general(rows, factor_b, over_columns, preferred_element_type=jnp.float32)
    rounded_proj = adapter_proj.astype(jnp.bfloat16)
    part_b = adapter_scale * lax.dot_general(low_rank, rows, over_slots, preferred_element_type=jnp.float32)
    proj_head = narrow(adapter_proj)
    both = jnp.concatenate([proj_head, narrow(adapter_proj - proj_head)], axis=1).astype(jnp.bfloat16)
    both = lax.dot_general(both, hidden, over_slots, preferred_element_type=jnp.float32)
    part_a = adapter_scale * (both[: factor_a.shape[0]] + both[factor_a.shape[0] :])
    over_y = sum_over_y(jnp.concatenate([part_b, part_a], axis=1))
    half_z = pair_sum(over_y, 1)
    summed = gather_over_y(pair_sum(half_z, lax.axis_size("dp") // Y_SIZE - 1)).astype(jnp.float32)

    projected = lax.dot_general(rows, weight, over_columns, preferred_element_type=jnp.float32)
    back = jnp.dot(rounded_proj, factor_a, preferred_element_type=jnp.float32)
    hidden_gradient = (projected + adapter_scale * back).astype(jnp.bfloat16)
    gate_terms = jnp.sum(hidden.astype(jnp.float32) * projected, axis=1)
    gate_terms = gate_terms + adapter_scale * jnp.sum(low_rank.astype(jnp.float32) * adapter_proj, axis=1)
    gate_terms, _ = lax.optimization_barrier((gate_terms, over_y))
    came_back = exchange(gate_terms.reshape(experts, capacity), "expert").reshape(-1)
    chosen = jnp.arange(slots, dtype=jnp.int32)[:, None] == slot_index
    gate_grad = jnp.sum(jnp.where(chosen, came_back[:, None], 0.0), axis=0) / gates
    return (hidden_gradient.reshape(saved_hidden.shape), gate_grad, summed[None, :, width:], summed[None, :, :width])


def solution(mesh):
    in_specs = (
        P(("dp", "expert"), None),
        P(("dp", "expert")),
        P(("dp", "expert")),
        P("dp", "expert", None, None),
        P("expert", None, None),
        P("expert", None, None),
        P("expert", None, None),
    )
    out_specs = (
        P("dp", "expert", None, None),
        P(("dp", "expert")),
        P("expert", None, None),
        P("expert", None, None),
    )
    return jax.shard_map(shards, mesh=mesh, in_specs=in_specs, out_specs=out_specs, check_vma=False)
```

```python
from functools import partial

import jax
import jax.numpy as jnp
from jax import lax
from jax.experimental import pallas as pl
from jax.experimental.pallas import tpu as pltpu
from jax.sharding import PartitionSpec as P

adapter_scale = 2.0
Y_SIZE = 4
SUBLANES = 8
LANES = 128
GRAD_PARTS = 4


def pack_kernel(capacity, ids_hbm, gate_hbm, grad_hbm, packed_ref, slot_ref, ids_ref, gate_ref, grad_ref, spread, sems):
    tokens, width = grad_ref.shape
    pieces, packed_rows, lanes = spread.shape
    slots = packed_rows // SUBLANES
    piece = width // SUBLANES
    small = [
        pltpu.make_async_copy(ids_hbm, ids_ref, sems.at[0]),
        pltpu.make_async_copy(gate_hbm, gate_ref, sems.at[1]),
    ]
    large = []
    for part in range(GRAD_PARTS):
        columns = pl.ds(part * (width // GRAD_PARTS), width // GRAD_PARTS)
        large.append(pltpu.make_async_copy(grad_hbm.at[:, columns], grad_ref.at[:, columns], sems.at[2 + part]))
    for copy in small + large:
        copy.start()
    for copy in small:
        copy.wait()
    ids = ids_ref[...]
    onehot = (lax.broadcasted_iota(jnp.int32, (slots // capacity, tokens), 0) == ids).astype(jnp.float32)
    earlier = lax.broadcasted_iota(jnp.int32, (tokens, tokens), 0) < lax.broadcasted_iota(jnp.int32, (tokens, tokens), 1)
    counts = jnp.dot(
        onehot.astype(jnp.bfloat16), earlier.astype(jnp.bfloat16), preferred_element_type=jnp.float32
    )
    token_rank = jnp.sum(onehot * counts, axis=0, keepdims=True).astype(jnp.int32)
    slot = ids * capacity + token_rank
    slot_ref[...] = slot
    gates = gate_ref[...].astype(jnp.float32)
    chosen = lax.broadcasted_iota(jnp.int32, (slots, tokens), 0) == slot
    select = jnp.where(chosen, gates, 0.0).astype(jnp.bfloat16)
    for j in range(SUBLANES):
        if j % (SUBLANES // GRAD_PARTS) == 0:
            large[j // (SUBLANES // GRAD_PARTS)].wait()
        rows = jnp.dot(select, grad_ref[:, j * piece : (j + 1) * piece], preferred_element_type=jnp.float32)
        for c in range(pieces):
            spread[c, pl.ds(j, slots, stride=SUBLANES), :] = rows[:, c * lanes : (c + 1) * lanes]
    for c in range(pieces):
        packed_ref[:, c * lanes : (c + 1) * lanes] = spread[c].astype(jnp.bfloat16)


def pack_rows(grad_out, expert_ids, gate_weight, slots, capacity):
    tokens, width = grad_out.shape
    piece = width // SUBLANES
    whole = pl.BlockSpec(memory_space=pltpu.VMEM)
    return pl.pallas_call(
        partial(pack_kernel, capacity),
        out_shape=(
            jax.ShapeDtypeStruct((slots * SUBLANES, piece), jnp.bfloat16),
            jax.ShapeDtypeStruct((1, tokens), jnp.int32),
        ),
        in_specs=[pl.BlockSpec(memory_space=pltpu.HBM)] * 3,
        out_specs=(whole, whole),
        scratch_shapes=[
            pltpu.VMEM((1, tokens), jnp.int32),
            pltpu.VMEM((1, tokens), jnp.bfloat16),
            pltpu.VMEM((tokens, width), jnp.bfloat16),
            pltpu.VMEM((piece // LANES, slots * SUBLANES, LANES), jnp.float32),
            pltpu.SemaphoreType.DMA((2 + GRAD_PARTS,)),
        ],
        compiler_params=pltpu.CompilerParams(vmem_limit_bytes=60 * 1024 * 1024),
        name="pack_rows",
    )(expert_ids.reshape(1, tokens), gate_weight.reshape(1, tokens), grad_out)


def exchange(blocks, axis, groups=None):
    return lax.all_to_all(blocks, axis, split_axis=0, concat_axis=0, tiled=True, axis_index_groups=groups)


def y_groups():
    z_count = lax.axis_size("dp") // Y_SIZE
    return [[z * Y_SIZE + y for y in range(Y_SIZE)] for z in range(z_count)]


def narrow(values):
    return lax.reduce_precision(values, exponent_bits=8, mantissa_bits=7)


def sum_over_y(part):
    rank = part.shape[0]
    mine = part.astype(jnp.bfloat16).reshape(Y_SIZE, rank // Y_SIZE, -1)
    return jnp.sum(exchange(mine, "dp", y_groups()).astype(jnp.float32), axis=0)


def pair_sum(part, masks):
    replicas, experts = lax.axis_size("dp"), lax.axis_size("expert")
    pairs = []
    for replica in range(replicas):
        z, y = divmod(replica, Y_SIZE)
        for expert in range(experts):
            partner = (z ^ masks[expert % 2]) * Y_SIZE + y
            pairs.append((replica * experts + expert, partner * experts + expert))
    own = narrow(part)
    other = lax.ppermute(own.astype(jnp.bfloat16), ("dp", "expert"), pairs)
    return own + other.astype(jnp.float32)


def gather_over_y(part):
    copies = jnp.broadcast_to(part.astype(jnp.bfloat16)[None], (Y_SIZE,) + part.shape)
    return exchange(copies, "dp", y_groups()).reshape(-1, part.shape[1])


def shards(grad_out, expert_ids, gate_weight, saved_hidden, down_weight, adapter_a, adapter_b):
    experts = lax.axis_size("expert")
    capacity = saved_hidden.shape[2] // experts
    slots = experts * capacity
    width = grad_out.shape[1]
    hidden_width = saved_hidden.shape[3]
    gates = gate_weight.astype(jnp.float32)
    packed, slot_index = pack_rows(grad_out, expert_ids, gate_weight, slots, capacity)
    arrived = exchange(packed.reshape(experts, capacity * SUBLANES, width // SUBLANES), "expert")
    rows = arrived.reshape(slots, width)

    hidden = saved_hidden.reshape(slots, hidden_width)
    weight, factor_a, factor_b = down_weight[0], adapter_a[0], adapter_b[0]
    low_rank = jnp.dot(hidden, factor_a.T, preferred_element_type=jnp.float32).astype(jnp.bfloat16)
    over_columns = (((1,), (1,)), ((), ()))
    over_slots = (((0,), (0,)), ((), ()))
    adapter_proj = lax.dot_general(rows, factor_b, over_columns, preferred_element_type=jnp.float32)
    rounded_proj = adapter_proj.astype(jnp.bfloat16)
    part_b = adapter_scale * lax.dot_general(low_rank, rows, over_slots, preferred_element_type=jnp.float32)
    proj_head = narrow(adapter_proj)
    both = jnp.concatenate([proj_head, narrow(adapter_proj - proj_head)], axis=1).astype(jnp.bfloat16)
    both = lax.dot_general(both, hidden, over_slots, preferred_element_type=jnp.float32)
    part_a = adapter_scale * (both[: factor_a.shape[0]] + both[factor_a.shape[0] :])
    over_y = sum_over_y(jnp.concatenate([part_b, part_a], axis=1))
    near, far = 1, lax.axis_size("dp") // Y_SIZE - 1
    half_z = pair_sum(over_y, (near, far))
    summed = gather_over_y(pair_sum(half_z, (far, near))).astype(jnp.float32)

    projected = lax.dot_general(rows, weight, over_columns, preferred_element_type=jnp.float32)
    back = jnp.dot(rounded_proj, factor_a, preferred_element_type=jnp.float32)
    hidden_gradient = (projected + adapter_scale * back).astype(jnp.bfloat16)
    gate_terms = jnp.sum(hidden.astype(jnp.float32) * projected, axis=1)
    gate_terms = gate_terms + adapter_scale * jnp.sum(low_rank.astype(jnp.float32) * adapter_proj, axis=1)
    gate_terms, _ = lax.optimization_barrier((gate_terms, over_y))
    came_back = exchange(gate_terms.reshape(experts, capacity), "expert").reshape(-1)
    chosen = jnp.arange(slots, dtype=jnp.int32)[:, None] == slot_index
    gate_grad = jnp.sum(jnp.where(chosen, came_back[:, None], 0.0), axis=0) / gates
    return (hidden_gradient.reshape(saved_hidden.shape), gate_grad, summed[None, :, width:], summed[None, :, :width])


def solution(mesh):
    in_specs = (
        P(("dp", "expert"), None),
        P(("dp", "expert")),
        P(("dp", "expert")),
        P("dp", "expert", None, None),
        P("expert", None, None),
        P("expert", None, None),
        P("expert", None, None),
    )
    out_specs = (
        P("dp", "expert", None, None),
        P(("dp", "expert")),
        P("expert", None, None),
        P("expert", None, None),
    )
    return jax.shard_map(shards, mesh=mesh, in_specs=in_specs, out_specs=out_specs, check_vma=False)
```

```python
from functools import partial

import jax
import jax.numpy as jnp
from jax import lax
from jax.experimental import pallas as pl
from jax.experimental.pallas import tpu as pltpu
from jax.sharding import PartitionSpec as P

adapter_scale = 2.0
Y_SIZE = 4
SUBLANES = 8
LANES = 128
GRAD_PARTS = 4


def pack_kernel(capacity, ids_hbm, gate_hbm, grad_hbm, packed_ref, slot_ref, ids_ref, gate_ref, grad_ref, spread, sems):
    tokens, width = grad_ref.shape
    pieces, packed_rows, lanes = spread.shape
    slots = packed_rows // SUBLANES
    piece = width // SUBLANES
    small = [
        pltpu.make_async_copy(ids_hbm, ids_ref, sems.at[0]),
        pltpu.make_async_copy(gate_hbm, gate_ref, sems.at[1]),
    ]
    large = []
    for part in range(GRAD_PARTS):
        columns = pl.ds(part * (width // GRAD_PARTS), width // GRAD_PARTS)
        large.append(pltpu.make_async_copy(grad_hbm.at[:, columns], grad_ref.at[:, columns], sems.at[2 + part]))
    for copy in small + large:
        copy.start()
    for copy in small:
        copy.wait()
    ids = ids_ref[...]
    onehot = (lax.broadcasted_iota(jnp.int32, (slots // capacity, tokens), 0) == ids).astype(jnp.float32)
    earlier = lax.broadcasted_iota(jnp.int32, (tokens, tokens), 0) < lax.broadcasted_iota(jnp.int32, (tokens, tokens), 1)
    counts = jnp.dot(
        onehot.astype(jnp.bfloat16), earlier.astype(jnp.bfloat16), preferred_element_type=jnp.float32
    )
    token_rank = jnp.sum(onehot * counts, axis=0, keepdims=True).astype(jnp.int32)
    slot = ids * capacity + token_rank
    slot_ref[...] = slot
    gates = gate_ref[...].astype(jnp.float32)
    chosen = lax.broadcasted_iota(jnp.int32, (slots, tokens), 0) == slot
    select = jnp.where(chosen, gates, 0.0).astype(jnp.bfloat16)
    for j in range(SUBLANES):
        if j % (SUBLANES // GRAD_PARTS) == 0:
            large[j // (SUBLANES // GRAD_PARTS)].wait()
        rows = jnp.dot(select, grad_ref[:, j * piece : (j + 1) * piece], preferred_element_type=jnp.float32)
        for c in range(pieces):
            spread[c, pl.ds(j, slots, stride=SUBLANES), :] = rows[:, c * lanes : (c + 1) * lanes]
    for c in range(pieces):
        packed_ref[:, c * lanes : (c + 1) * lanes] = spread[c].astype(jnp.bfloat16)


def pack_rows(grad_out, expert_ids, gate_weight, slots, capacity):
    tokens, width = grad_out.shape
    piece = width // SUBLANES
    whole = pl.BlockSpec(memory_space=pltpu.VMEM)
    return pl.pallas_call(
        partial(pack_kernel, capacity),
        out_shape=(
            jax.ShapeDtypeStruct((slots * SUBLANES, piece), jnp.bfloat16),
            jax.ShapeDtypeStruct((1, tokens), jnp.int32),
        ),
        in_specs=[pl.BlockSpec(memory_space=pltpu.HBM)] * 3,
        out_specs=(whole, whole),
        scratch_shapes=[
            pltpu.VMEM((1, tokens), jnp.int32),
            pltpu.VMEM((1, tokens), jnp.bfloat16),
            pltpu.VMEM((tokens, width), jnp.bfloat16),
            pltpu.VMEM((piece // LANES, slots * SUBLANES, LANES), jnp.float32),
            pltpu.SemaphoreType.DMA((2 + GRAD_PARTS,)),
        ],
        compiler_params=pltpu.CompilerParams(vmem_limit_bytes=60 * 1024 * 1024),
        name="pack_rows",
    )(expert_ids.reshape(1, tokens), gate_weight.reshape(1, tokens), grad_out)


def last_sum_kernel(width, own_ref, other_ref, copies_ref):
    columns = own_ref.shape[1]
    total = own_ref[...] + other_ref[...].astype(jnp.float32)
    head = total.astype(jnp.bfloat16)
    rest = (total[:, width:] - head[:, width:].astype(jnp.float32)).astype(jnp.bfloat16)
    for copy in range(copies_ref.shape[0]):
        copies_ref[copy, :, :columns] = head
        copies_ref[copy, :, columns:] = rest


def last_sum(own, other, copies, width):
    rank, columns = own.shape
    whole = pl.BlockSpec(memory_space=pltpu.VMEM)
    return pl.pallas_call(
        partial(last_sum_kernel, width),
        out_shape=jax.ShapeDtypeStruct((copies, rank, 2 * columns - width), jnp.bfloat16),
        in_specs=[whole] * 2,
        out_specs=whole,
        compiler_params=pltpu.CompilerParams(vmem_limit_bytes=8 * 1024 * 1024),
        name="last_sum",
    )(own, other)


def widen_kernel(both_ref, factor_b_ref, factor_a_ref):
    width = factor_b_ref.shape[1]
    columns = width + factor_a_ref.shape[1]
    factor_b_ref[...] = both_ref[:, :width].astype(jnp.float32)
    factor_a_ref[...] = both_ref[:, width:columns].astype(jnp.float32) + both_ref[:, columns:].astype(jnp.float32)


def widen(both, width):
    rank, columns = both.shape
    whole = pl.BlockSpec(memory_space=pltpu.VMEM)
    return pl.pallas_call(
        widen_kernel,
        out_shape=(
            jax.ShapeDtypeStruct((rank, width), jnp.float32),
            jax.ShapeDtypeStruct((rank, (columns - width) // 2), jnp.float32),
        ),
        in_specs=[whole],
        out_specs=(whole, whole),
        compiler_params=pltpu.CompilerParams(vmem_limit_bytes=8 * 1024 * 1024),
        name="widen",
    )(both)


def exchange(blocks, axis, groups=None):
    return lax.all_to_all(blocks, axis, split_axis=0, concat_axis=0, tiled=True, axis_index_groups=groups)


def y_groups():
    z_count = lax.axis_size("dp") // Y_SIZE
    return [[z * Y_SIZE + y for y in range(Y_SIZE)] for z in range(z_count)]


def narrow(values):
    return lax.reduce_precision(values, exponent_bits=8, mantissa_bits=7)


def sum_over_y(part):
    rank = part.shape[0]
    mine = part.astype(jnp.bfloat16).reshape(Y_SIZE, rank // Y_SIZE, -1)
    return jnp.sum(exchange(mine, "dp", y_groups()).astype(jnp.float32), axis=0)


def with_pair(part, masks):
    replicas, experts = lax.axis_size("dp"), lax.axis_size("expert")
    pairs = []
    for replica in range(replicas):
        z, y = divmod(replica, Y_SIZE)
        for expert in range(experts):
            partner = (z ^ masks[expert % 2]) * Y_SIZE + y
            pairs.append((replica * experts + expert, partner * experts + expert))
    own = narrow(part)
    return own, lax.ppermute(own.astype(jnp.bfloat16), ("dp", "expert"), pairs)


def shards(grad_out, expert_ids, gate_weight, saved_hidden, down_weight, adapter_a, adapter_b):
    experts = lax.axis_size("expert")
    capacity = saved_hidden.shape[2] // experts
    slots = experts * capacity
    width = grad_out.shape[1]
    hidden_width = saved_hidden.shape[3]
    gates = gate_weight.astype(jnp.float32)
    packed, slot_index = pack_rows(grad_out, expert_ids, gate_weight, slots, capacity)
    arrived = exchange(packed.reshape(experts, capacity * SUBLANES, width // SUBLANES), "expert")
    rows = arrived.reshape(slots, width)

    hidden = saved_hidden.reshape(slots, hidden_width)
    weight, factor_a, factor_b = down_weight[0], adapter_a[0], adapter_b[0]
    low_rank = jnp.dot(hidden, factor_a.T, preferred_element_type=jnp.float32).astype(jnp.bfloat16)
    over_columns = (((1,), (1,)), ((), ()))
    over_slots = (((0,), (0,)), ((), ()))
    adapter_proj = lax.dot_general(rows, factor_b, over_columns, preferred_element_type=jnp.float32)
    rounded_proj = adapter_proj.astype(jnp.bfloat16)
    part_b = adapter_scale * lax.dot_general(low_rank, rows, over_slots, preferred_element_type=jnp.float32)
    proj_head = narrow(adapter_proj)
    both = jnp.concatenate([proj_head, narrow(adapter_proj - proj_head)], axis=1).astype(jnp.bfloat16)
    both = lax.dot_general(both, hidden, over_slots, preferred_element_type=jnp.float32)
    part_a = adapter_scale * (both[: factor_a.shape[0]] + both[factor_a.shape[0] :])
    over_y = sum_over_y(jnp.concatenate([part_b, part_a], axis=1))
    near, far = 1, lax.axis_size("dp") // Y_SIZE - 1
    own, other = with_pair(over_y, (near, far))
    own, other = with_pair(own + other.astype(jnp.float32), (far, near))
    summed = exchange(last_sum(own, other, Y_SIZE, width), "dp", y_groups())
    grad_b, grad_a = widen(summed.reshape(factor_b.shape[0], -1), width)

    projected = lax.dot_general(rows, weight, over_columns, preferred_element_type=jnp.float32)
    back = jnp.dot(rounded_proj, factor_a, preferred_element_type=jnp.float32)
    hidden_gradient = (projected + adapter_scale * back).astype(jnp.bfloat16)
    gate_terms = jnp.sum(hidden.astype(jnp.float32) * projected, axis=1)
    gate_terms = gate_terms + adapter_scale * jnp.sum(low_rank.astype(jnp.float32) * adapter_proj, axis=1)
    gate_terms, _ = lax.optimization_barrier((gate_terms, over_y))
    came_back = exchange(gate_terms.reshape(experts, capacity), "expert").reshape(-1)
    chosen = jnp.arange(slots, dtype=jnp.int32)[:, None] == slot_index
    gate_grad = jnp.sum(jnp.where(chosen, came_back[:, None], 0.0), axis=0) / gates
    return (hidden_gradient.reshape(saved_hidden.shape), gate_grad, grad_a[None], grad_b[None])


def solution(mesh):
    in_specs = (
        P(("dp", "expert"), None),
        P(("dp", "expert")),
        P(("dp", "expert")),
        P("dp", "expert", None, None),
        P("expert", None, None),
        P("expert", None, None),
        P("expert", None, None),
    )
    out_specs = (
        P("dp", "expert", None, None),
        P(("dp", "expert")),
        P("expert", None, None),
        P("expert", None, None),
    )
    return jax.shard_map(shards, mesh=mesh, in_specs=in_specs, out_specs=out_specs, check_vma=False)
```

```python
from functools import partial

import jax
import jax.numpy as jnp
from jax import lax
from jax.experimental import pallas as pl
from jax.experimental.pallas import tpu as pltpu
from jax.sharding import PartitionSpec as P

adapter_scale = 2.0
Y_SIZE = 4
SUBLANES = 8
LANES = 128
GRAD_PARTS = 8


def pack_kernel(capacity, ids_hbm, gate_hbm, grad_hbm, packed_ref, slot_ref, ids_ref, gate_ref, grad_ref, spread, sems):
    tokens, width = grad_ref.shape
    pieces, packed_rows, lanes = spread.shape
    slots = packed_rows // SUBLANES
    piece = width // SUBLANES
    small = [
        pltpu.make_async_copy(ids_hbm, ids_ref, sems.at[0]),
        pltpu.make_async_copy(gate_hbm, gate_ref, sems.at[1]),
    ]
    large = []
    for part in range(GRAD_PARTS):
        columns = pl.ds(part * (width // GRAD_PARTS), width // GRAD_PARTS)
        large.append(pltpu.make_async_copy(grad_hbm.at[:, columns], grad_ref.at[:, columns], sems.at[2 + part]))
    for copy in small + large:
        copy.start()
    for copy in small:
        copy.wait()
    ids = ids_ref[...]
    onehot = (lax.broadcasted_iota(jnp.int32, (slots // capacity, tokens), 0) == ids).astype(jnp.float32)
    earlier = lax.broadcasted_iota(jnp.int32, (tokens, tokens), 0) < lax.broadcasted_iota(jnp.int32, (tokens, tokens), 1)
    counts = jnp.dot(
        onehot.astype(jnp.bfloat16), earlier.astype(jnp.bfloat16), preferred_element_type=jnp.float32
    )
    token_rank = jnp.sum(onehot * counts, axis=0, keepdims=True).astype(jnp.int32)
    slot = ids * capacity + token_rank
    slot_ref[...] = slot
    gates = gate_ref[...].astype(jnp.float32)
    chosen = lax.broadcasted_iota(jnp.int32, (slots, tokens), 0) == slot
    select = jnp.where(chosen, gates, 0.0).astype(jnp.bfloat16)
    for j in range(SUBLANES):
        if j % (SUBLANES // GRAD_PARTS) == 0:
            large[j // (SUBLANES // GRAD_PARTS)].wait()
        rows = jnp.dot(select, grad_ref[:, j * piece : (j + 1) * piece], preferred_element_type=jnp.float32)
        for c in range(pieces):
            spread[c, pl.ds(j, slots, stride=SUBLANES), :] = rows[:, c * lanes : (c + 1) * lanes]
    for c in range(pieces):
        packed_ref[:, c * lanes : (c + 1) * lanes] = spread[c].astype(jnp.bfloat16)


def pack_rows(grad_out, expert_ids, gate_weight, slots, capacity):
    tokens, width = grad_out.shape
    piece = width // SUBLANES
    whole = pl.BlockSpec(memory_space=pltpu.VMEM)
    return pl.pallas_call(
        partial(pack_kernel, capacity),
        out_shape=(
            jax.ShapeDtypeStruct((slots * SUBLANES, piece), jnp.bfloat16),
            jax.ShapeDtypeStruct((1, tokens), jnp.int32),
        ),
        in_specs=[pl.BlockSpec(memory_space=pltpu.HBM)] * 3,
        out_specs=(whole, whole),
        scratch_shapes=[
            pltpu.VMEM((1, tokens), jnp.int32),
            pltpu.VMEM((1, tokens), jnp.bfloat16),
            pltpu.VMEM((tokens, width), jnp.bfloat16),
            pltpu.VMEM((piece // LANES, slots * SUBLANES, LANES), jnp.float32),
            pltpu.SemaphoreType.DMA((2 + GRAD_PARTS,)),
        ],
        compiler_params=pltpu.CompilerParams(vmem_limit_bytes=60 * 1024 * 1024),
        name="pack_rows",
    )(expert_ids.reshape(1, tokens), gate_weight.reshape(1, tokens), grad_out)


def last_sum_kernel(width, own_ref, other_ref, copies_ref):
    columns = own_ref.shape[1]
    total = own_ref[...] + other_ref[...].astype(jnp.float32)
    head = total.astype(jnp.bfloat16)
    rest = (total[:, width:] - head[:, width:].astype(jnp.float32)).astype(jnp.bfloat16)
    for copy in range(copies_ref.shape[0]):
        copies_ref[copy, :, :columns] = head
        copies_ref[copy, :, columns:] = rest


def last_sum(own, other, copies, width):
    rank, columns = own.shape
    whole = pl.BlockSpec(memory_space=pltpu.VMEM)
    return pl.pallas_call(
        partial(last_sum_kernel, width),
        out_shape=jax.ShapeDtypeStruct((copies, rank, 2 * columns - width), jnp.bfloat16),
        in_specs=[whole] * 2,
        out_specs=whole,
        compiler_params=pltpu.CompilerParams(vmem_limit_bytes=8 * 1024 * 1024),
        name="last_sum",
    )(own, other)


def widen_kernel(both_ref, factor_b_ref, factor_a_ref):
    width = factor_b_ref.shape[1]
    columns = width + factor_a_ref.shape[1]
    factor_b_ref[...] = both_ref[:, :width].astype(jnp.float32)
    factor_a_ref[...] = both_ref[:, width:columns].astype(jnp.float32) + both_ref[:, columns:].astype(jnp.float32)


def widen(both, width):
    rank, columns = both.shape
    whole = pl.BlockSpec(memory_space=pltpu.VMEM)
    return pl.pallas_call(
        widen_kernel,
        out_shape=(
            jax.ShapeDtypeStruct((rank, width), jnp.float32),
            jax.ShapeDtypeStruct((rank, (columns - width) // 2), jnp.float32),
        ),
        in_specs=[whole],
        out_specs=(whole, whole),
        compiler_params=pltpu.CompilerParams(vmem_limit_bytes=8 * 1024 * 1024),
        name="widen",
    )(both)


def exchange(blocks, axis, groups=None):
    return lax.all_to_all(blocks, axis, split_axis=0, concat_axis=0, tiled=True, axis_index_groups=groups)


def y_groups():
    z_count = lax.axis_size("dp") // Y_SIZE
    return [[z * Y_SIZE + y for y in range(Y_SIZE)] for z in range(z_count)]


def narrow(values):
    return lax.reduce_precision(values, exponent_bits=8, mantissa_bits=7)


def sum_over_y(part):
    rank = part.shape[0]
    mine = part.astype(jnp.bfloat16).reshape(Y_SIZE, rank // Y_SIZE, -1)
    return jnp.sum(exchange(mine, "dp", y_groups()).astype(jnp.float32), axis=0)


def with_pair(part, masks):
    replicas, experts = lax.axis_size("dp"), lax.axis_size("expert")
    pairs = []
    for replica in range(replicas):
        z, y = divmod(replica, Y_SIZE)
        for expert in range(experts):
            partner = (z ^ masks[expert % 2]) * Y_SIZE + y
            pairs.append((replica * experts + expert, partner * experts + expert))
    own = narrow(part)
    return own, lax.ppermute(own.astype(jnp.bfloat16), ("dp", "expert"), pairs)


def shards(grad_out, expert_ids, gate_weight, saved_hidden, down_weight, adapter_a, adapter_b):
    experts = lax.axis_size("expert")
    capacity = saved_hidden.shape[2] // experts
    slots = experts * capacity
    width = grad_out.shape[1]
    hidden_width = saved_hidden.shape[3]
    gates = gate_weight.astype(jnp.float32)
    packed, slot_index = pack_rows(grad_out, expert_ids, gate_weight, slots, capacity)
    arrived = exchange(packed.reshape(experts, capacity * SUBLANES, width // SUBLANES), "expert")
    rows = arrived.reshape(slots, width)

    hidden = saved_hidden.reshape(slots, hidden_width)
    weight, factor_a, factor_b = down_weight[0], adapter_a[0], adapter_b[0]
    low_rank = jnp.dot(hidden, factor_a.T, preferred_element_type=jnp.float32).astype(jnp.bfloat16)
    over_columns = (((1,), (1,)), ((), ()))
    over_slots = (((0,), (0,)), ((), ()))
    adapter_proj = lax.dot_general(rows, factor_b, over_columns, preferred_element_type=jnp.float32)
    rounded_proj = adapter_proj.astype(jnp.bfloat16)
    part_b = adapter_scale * lax.dot_general(low_rank, rows, over_slots, preferred_element_type=jnp.float32)
    proj_head = narrow(adapter_proj)
    both = jnp.concatenate([proj_head, narrow(adapter_proj - proj_head)], axis=1).astype(jnp.bfloat16)
    both = lax.dot_general(both, hidden, over_slots, preferred_element_type=jnp.float32)
    part_a = adapter_scale * (both[: factor_a.shape[0]] + both[factor_a.shape[0] :])
    over_y = sum_over_y(jnp.concatenate([part_b, part_a], axis=1))
    near, far = 1, lax.axis_size("dp") // Y_SIZE - 1
    own, other = with_pair(over_y, (far, near))
    own, other = with_pair(own + other.astype(jnp.float32), (near, far))
    summed = exchange(last_sum(own, other, Y_SIZE, width), "dp", y_groups())
    grad_b, grad_a = widen(summed.reshape(factor_b.shape[0], -1), width)

    projected = lax.dot_general(rows, weight, over_columns, preferred_element_type=jnp.float32)
    back = jnp.dot(rounded_proj, factor_a, preferred_element_type=jnp.float32)
    hidden_gradient = (projected + adapter_scale * back).astype(jnp.bfloat16)
    gate_terms = jnp.sum(hidden.astype(jnp.float32) * projected, axis=1)
    gate_terms = gate_terms + adapter_scale * jnp.sum(low_rank.astype(jnp.float32) * adapter_proj, axis=1)
    gate_terms, _ = lax.optimization_barrier((gate_terms, over_y))
    came_back = exchange(gate_terms.reshape(experts, capacity), "expert").reshape(-1)
    chosen = jnp.arange(slots, dtype=jnp.int32)[:, None] == slot_index
    gate_grad = jnp.sum(jnp.where(chosen, came_back[:, None], 0.0), axis=0) / gates
    return (hidden_gradient.reshape(saved_hidden.shape), gate_grad, grad_a[None], grad_b[None])


def solution(mesh):
    in_specs = (
        P(("dp", "expert"), None),
        P(("dp", "expert")),
        P(("dp", "expert")),
        P("dp", "expert", None, None),
        P("expert", None, None),
        P("expert", None, None),
        P("expert", None, None),
    )
    out_specs = (
        P("dp", "expert", None, None),
        P(("dp", "expert")),
        P("expert", None, None),
        P("expert", None, None),
    )
    return jax.shard_map(shards, mesh=mesh, in_specs=in_specs, out_specs=out_specs, check_vma=False)
```
